256 devices in a mesh: grp: 32 (over z, y), tp: 8 (over x, core).
Axes of the slice: x: 4, y: 4, z: 8, core: 2. Of those that a mesh axis runs over, the one named last changes fastest.
Arguments:
- queries: bfloat16 [32, 64, 128], P('grp', 'tp'), may hold values from -12 to 12
- new_keys: bfloat16 [32, 8, 128], P('grp', 'tp'), may hold values from -6 to 6
- new_values: bfloat16 [32, 8, 128], P('grp', 'tp'), may hold values from -6 to 6
- key_cache: bfloat16 [3072, 8, 256, 128], P('grp', 'tp'), may hold values from -6 to 6
- paged_value_cache: bfloat16 [3072, 8, 256, 128], P('grp', 'tp'), may hold values from -6 to 6
- lengths: int32 [32], replicated, may hold values from 1 to 36864, as said below
- placement: int32 [3072, 2], P('grp'), may hold values from 0 to 143, as said below
- out_weight: bfloat16 [8192, 8192], P('tp', 'grp'), may hold values from -0.1875 to 0.1875
Outputs:
- projected: bfloat16 [32, 8192], P(None, ('grp', 'tp'))
The draws below stay inside these ranges and needn't reach their ends.
Inputs may be any that keep to these rules, and one draw needn't show every extreme that they name: Request r's blocks are numbered 0 to ceil(lengths[r] / 256) - 1. `placement`: row i is slot i, rows of group g being g * 96 to (g + 1) * 96 - 1; first column: the owning request, 32 for an empty slot; second column: the block's number (0 in an empty slot); every block of every request stands in exactly one slot.
All inputs are finite; a program needn't handle non-finite values.
Results may differ from the reference program's by a relative error of at most 0.0048.
Values may be sent and summed in bfloat16 or wider, within the bound.
A program may use at most 64 MiB of HBM per device.

```python
import jax
import jax.numpy as jnp
from jax import lax

D = 8192
HQ = 64
KEY_VALUE_HEADS = 8
HEAD_SIZE = 128
BLOCK_TOKENS = 256
SLOTS = 96
REQ_GRP = 1
REQUESTS = 32
SLOT_TOTAL = 3072
N_GRP = 32


def blocks_plan(key):
    first_part, second_part, third_part, fourth = jax.random.split(key, 4)
    weights = jax.random.randint(first_part, (REQUESTS,), 1, 17)
    target_group = SLOT_TOTAL * 3 // 4
    most_blocks = 3 * SLOTS // (2 * REQ_GRP)
    spare = target_group - REQUESTS - most_blocks
    counts = 1 + jnp.minimum(most_blocks - 1, weights * spare // jnp.sum(weights))
    extra = jax.random.randint(second_part, (REQUESTS,), 1, BLOCK_TOKENS + 1)
    longest = jax.random.randint(fourth, (), 0, REQUESTS)
    shortest = (longest + 1) % REQUESTS
    counts = counts.at[longest].set(most_blocks).at[shortest].set(1)
    extra = extra.at[longest].set(BLOCK_TOKENS).at[shortest].set(1)
    ends = jnp.cumsum(counts)
    starts = ends - counts
    lengths = ((counts - 1) * BLOCK_TOKENS + extra).astype(jnp.int32)
    sort_order = jax.random.permutation(third_part, SLOT_TOTAL)
    rank_positions = jnp.arange(SLOT_TOTAL, dtype=jnp.int32)
    owner_groups = jnp.sum((rank_positions[:, None] >= ends[None, :]).astype(jnp.int32), 1)
    clamped = jnp.minimum(owner_groups, REQUESTS - 1)
    block_numbers = jnp.where(owner_groups < REQUESTS, rank_positions - jnp.take(starts, clamped), 0)
    owner_of_slot = jnp.zeros((SLOT_TOTAL,), jnp.int32).at[sort_order].set(owner_groups.astype(jnp.int32))
    block_of_slot = jnp.zeros((SLOT_TOTAL,), jnp.int32).at[sort_order].set(block_numbers.astype(jnp.int32))
    return (lengths, jnp.stack([owner_of_slot, block_of_slot], 1))


def draw_lengths(key, part):
    lengths, table = blocks_plan(key)
    return lengths


def draw_placement(key, part):
    lengths, table = blocks_plan(key)
    return table


def draw_queries(key, part):
    key = jax.random.fold_in(key, 11)
    first_part = jax.random.fold_in(key, 0)
    value_rows = 2.5 * jax.random.normal(first_part, (REQUESTS, HQ, HEAD_SIZE), jnp.float32)
    return jnp.clip(value_rows, -12.0, 12.0).astype(jnp.bfloat16)


def draw_key_cache(key, part):
    key = jax.random.fold_in(key, 23)
    first_part = jax.random.fold_in(key, 0)
    value_rows = jax.random.normal(first_part, (SLOT_TOTAL, KEY_VALUE_HEADS, BLOCK_TOKENS, HEAD_SIZE), jnp.float32)
    return jnp.clip(value_rows, -6.0, 6.0).astype(jnp.bfloat16)


def block_scale(key, extent, pieces, least, largest):
    def one(axis_at, blocks):
        draws = jax.random.uniform(jax.random.fold_in(jax.random.fold_in(key, 6), axis_at), (blocks,), jnp.float32, least / len(pieces), largest / len(pieces))
        return jnp.repeat(jnp.exp(draws), extent[axis_at] // blocks).reshape((-1,) + (1,) * (len(extent) - axis_at - 1))

    gain = one(*pieces[0])
    for cut in pieces[1:]:
        gain = gain * one(*cut)
    return gain


def noise(key, shape, scale, bound, pieces=(), held_as=jnp.bfloat16):
    array = scale * jax.random.normal(key, shape, jnp.float32)
    if pieces:
        array = array * block_scale(key, shape, pieces, -0.22, 0.18)
    return jnp.clip(array, -bound, bound).astype(held_as)


def setup_inputs(seed: int = 0) -> dict:
    seeds = jax.random.split(jax.random.key(seed), 9)
    queries = draw_queries(jax.random.fold_in(seeds[8], 71), 0)
    new_keys = noise(seeds[1], (REQUESTS, KEY_VALUE_HEADS, HEAD_SIZE), 1.0, 6.0, ((0, 32), (1, 8)))
    new_values = noise(seeds[2], (REQUESTS, KEY_VALUE_HEADS, HEAD_SIZE), 1.0, 6.0, ((0, 32), (1, 8)))
    key_cache = draw_key_cache(jax.random.fold_in(seeds[8], 71), 0)
    paged_value_cache = noise(seeds[4], (SLOT_TOTAL, KEY_VALUE_HEADS, BLOCK_TOKENS, HEAD_SIZE), 1.0, 6.0, ((0, 32), (1, 8)))
    lengths = draw_lengths(jax.random.fold_in(seeds[8], 71), 0)
    placement = draw_placement(jax.random.fold_in(seeds[8], 71), 0)
    out_weight = noise(seeds[7], (HQ * HEAD_SIZE, D), (D // 8) ** -0.5, 0.1875, ((0, 8), (1, 32)))
    return {"queries": queries, "new_keys": new_keys, "new_values": new_values, "key_cache": key_cache, "paged_value_cache": paged_value_cache, "lengths": lengths, "placement": placement, "out_weight": out_weight}


very_negative = -1.0e30


def slot_terms(q_all, keys, value_rows, placement, lengths):
    req_count = q_all.shape[0]
    slot_count, kv_heads, block_len, head_dim = keys.shape
    group_size = q_all.shape[1] // kv_heads
    score_scale = head_dim ** -0.5
    owner_groups = placement[:, 0]
    block_numbers = placement[:, 1]
    onehot = owner_groups[:, None] == jnp.arange(req_count, dtype=jnp.int32)[None, :]
    picked = jnp.dot(onehot.astype(jnp.bfloat16), q_all.reshape(req_count, -1), preferred_element_type=jnp.float32)
    picked = picked.reshape(slot_count, kv_heads, group_size, head_dim)
    clamped = jnp.minimum(owner_groups, req_count - 1).astype(jnp.int32)
    live_len = jnp.take(lengths, clamped)
    positions = block_numbers[:, None] * block_len + jnp.arange(block_len, dtype=jnp.int32)[None, :]
    live_mask = (positions < live_len[:, None]) & (owner_groups < req_count)[:, None]
    scores = jnp.einsum('skgd,skbd->skgb', picked, keys.astype(jnp.float32)) * score_scale
    scores = jnp.where(live_mask[:, None, None, :], scores, very_negative)
    maxima = jnp.max(scores, -1)
    weights = jnp.exp(scores - maxima[..., None]) * live_mask[:, None, None, :].astype(jnp.float32)
    totals = jnp.sum(weights, -1)
    weights_bf = weights.astype(jnp.bfloat16).astype(jnp.float32)
    mixture = jnp.einsum('skgb,skbd->skgd', weights_bf, value_rows.astype(jnp.float32))
    best = jnp.max(jnp.where(onehot[:, :, None, None], maxima[:, None], very_negative), 0)
    factor = jnp.exp(maxima - jnp.take(best, clamped, axis=0)) * (owner_groups < req_count)[:, None, None].astype(jnp.float32)
    onef = onehot.astype(jnp.float32)
    weight_sum = jnp.einsum('sr,skg->rkg', onef, totals * factor, precision=lax.Precision.HIGHEST)
    value_sum = jnp.einsum('sr,skgd->rkgd', onef, mixture * factor[..., None], precision=lax.Precision.HIGHEST)
    return best, weight_sum, value_sum


def home_combine(maxima, totals, sums, new_score, new_values):
    summit = jnp.maximum(jnp.max(maxima, 1), new_score)
    scaled = jnp.exp(maxima - summit[:, None])
    own_term = jnp.exp(new_score - summit)
    total = jnp.sum(totals * scaled, 1) + own_term
    summed = jnp.sum(sums * scaled[..., None], 1) + own_term[..., None] * new_values[:, :, None, :].astype(jnp.float32)
    return summed / total[..., None]


def reference(queries, new_keys, new_values, key_cache, paged_value_cache, lengths, placement, out_weight):
    group_size = HQ // KEY_VALUE_HEADS
    grouped_keys = key_cache.reshape(N_GRP, SLOTS, KEY_VALUE_HEADS, BLOCK_TOKENS, HEAD_SIZE)
    grouped_values = paged_value_cache.reshape(N_GRP, SLOTS, KEY_VALUE_HEADS, BLOCK_TOKENS, HEAD_SIZE)
    grouped_place = placement.reshape(N_GRP, SLOTS, 2)

    def one_group(items):
        return slot_terms(queries, items[0], items[1], items[2], lengths)

    maxima, totals, sums = lax.map(one_group, (grouped_keys, grouped_values, grouped_place))
    maxima = jnp.moveaxis(maxima, 0, 1)
    totals = jnp.moveaxis(totals, 0, 1)
    sums = jnp.moveaxis(sums, 0, 1)
    grouped_q = queries.reshape(REQUESTS, KEY_VALUE_HEADS, group_size, HEAD_SIZE).astype(jnp.float32)
    new_score = jnp.einsum('rkgd,rkd->rkg', grouped_q, new_keys.astype(jnp.float32)) * (HEAD_SIZE ** -0.5)
    attention = home_combine(maxima, totals, sums, new_score, new_values)
    attention = attention.reshape(REQUESTS, HQ * HEAD_SIZE).astype(jnp.bfloat16)
    return jnp.dot(attention, out_weight, preferred_element_type=jnp.float32).astype(jnp.bfloat16)
```

```python
import functools
import math

import jax
import jax.numpy as jnp
from jax import lax
from jax.experimental import pallas as pl
from jax.experimental.pallas import tpu as pltpu
from jax.sharding import PartitionSpec as P

MESH = pl.DeviceIdType.MESH
NEG = -1e30
F32 = jnp.float32
BF16 = jnp.bfloat16


def hops(offset, z_extent, y_extent):
    z, y = offset // y_extent, offset % y_extent
    return min(z, z_extent - z) + min(y, y_extent - y)


def kernel(
    grp_count,
    tp_count,
    q_hbm,
    nk_hbm,
    nv_hbm,
    k_hbm,
    v_hbm,
    len_ref,
    place_ref,
    w_hbm,
    out_ref,
    q_all,
    nk,
    nv,
    keys,
    vals,
    w,
    q_sel,
    scores,
    group_max,
    mix,
    tot,
    msg_f,
    msg,
    got,
    att,
    att_f,
    part_out,
    part_in,
    sem_small,
    sem_k,
    sem_v,
    sem_w,
    send_sems,
    recv_sems,
):
    g = lax.axis_index("grp")
    t = lax.axis_index("tp")
    slots, tokens, head = keys.shape
    heads = q_all.shape[1]
    scale = head**-0.5 * math.log2(math.e)

    order = sorted(range(1, grp_count), key=lambda i: -hops(i, grp_count // 4, 4))
    tp_order = sorted(range(1, tp_count), key=lambda i: -min(i, tp_count - i))

    def grp_peer(i):
        return lax.rem(g + i, grp_count)

    def tp_peer(i):
        return lax.rem(t + i, tp_count)

    barrier = pltpu.get_barrier_semaphore()
    for i in order:
        pl.semaphore_signal(barrier, 1, device_id={"grp": grp_peer(i)}, device_id_type=MESH)
    for i in tp_order:
        pl.semaphore_signal(barrier, 1, device_id={"tp": tp_peer(i)}, device_id_type=MESH)

    small = [
        pltpu.make_async_copy(q_hbm.at[0], q_all.at[g], sem_small.at[0]),
        pltpu.make_async_copy(nk_hbm.at[0], nk, sem_small.at[1]),
        pltpu.make_async_copy(nv_hbm.at[0], nv, sem_small.at[2]),
    ]
    for c in small:
        c.start()
    big = [
        pltpu.make_async_copy(k_hbm, keys, sem_k),
        pltpu.make_async_copy(v_hbm, vals, sem_v),
        pltpu.make_async_copy(w_hbm, w, sem_w),
    ]
    for c in big:
        c.start()
    for c in small:
        c.wait()

    lane = lax.broadcasted_iota(jnp.int32, (heads, 128), 1)
    row = lax.broadcasted_iota(jnp.int32, (grp_count, 128), 0)
    token = lax.broadcasted_iota(jnp.int32, (heads, tokens), 1)

    owner_row = jnp.full((heads, 128), grp_count, jnp.int32)
    for s in range(slots):
        owner_row = jnp.where(lane == s, place_ref[s, 0], owner_row)
    onehot = jnp.where(owner_row[:1, :] == row, 1.0, 0.0)[:, :slots].astype(BF16)
    onehot2 = jnp.concatenate([onehot, onehot], axis=1)

    pl.semaphore_wait(barrier, grp_count - 1 + tp_count - 1)
    for i in order:
        pltpu.make_async_remote_copy(
            q_all.at[g],
            q_all.at[g],
            send_sems.at[0],
            recv_sems.at[0],
            device_id={"grp": grp_peer(i)},
            device_id_type=MESH,
        ).start()
    big[0].wait()
    others = q_all.at[pl.ds(0, grp_count - 1)]
    pltpu.make_async_copy(others, others, recv_sems.at[0]).wait()

    chunk = 24
    for c in range(slots // chunk):
        for s in range(c * chunk, (c + 1) * chunk):
            q_sel[s] = q_all[jnp.minimum(place_ref[s, 0], grp_count - 1)]
    slot_max = jnp.full((heads, 128), NEG, F32)
    for s in range(slots):
        owner = place_ref[s, 0]
        live = len_ref[jnp.minimum(owner, grp_count - 1)] - place_ref[s, 1] * tokens
        live = jnp.where(owner < grp_count, live, 0)
        x = lax.dot_general(
            q_sel[s], keys[s], (((1,), (1,)), ((), ())), preferred_element_type=F32
        )
        x = jnp.where(token < live, x * scale, NEG)
        scores[s] = x
        slot_max = jnp.where(lane == s, jnp.max(x, axis=1, keepdims=True), slot_max)
    for r in range(grp_count):
        top = jnp.max(jnp.where(owner_row == r, slot_max, NEG), axis=1, keepdims=True)
        group_max[r] = jnp.broadcast_to(top, (heads, 128))

    ones = jnp.ones((tokens, 128), BF16)
    big[1].wait()
    for s in range(slots):
        top = group_max[jnp.minimum(place_ref[s, 0], grp_count - 1)]
        p = jnp.exp2(scores[s] - jnp.concatenate([top, top], axis=1)).astype(BF16)
        mix[s] = jnp.dot(p, vals[s], preferred_element_type=F32)
        tot[s] = jnp.dot(p, ones, preferred_element_type=F32)

    lane_r = lax.broadcasted_iota(jnp.int32, (grp_count, 128), 1)
    for h in range(heads):
        both = jnp.concatenate([mix[:, h, :], tot[:, h, :]], axis=1)
        hi = both.astype(BF16)
        lo = (both - hi.astype(F32)).astype(BF16)
        sums = jnp.dot(onehot2, jnp.concatenate([hi, lo], axis=0), preferred_element_type=F32)
        value_sum, weight_sum = sums[:, :128], sums[:, 128:]
        there = weight_sum > 0.0
        safe = jnp.where(there, weight_sum, 1.0)
        norm = value_sum / safe
        lse = jnp.where(there, group_max[:, h, :] + jnp.log2(safe), NEG)
        first = lse.astype(BF16).astype(F32)
        rest = lse - first
        second = rest.astype(BF16).astype(F32)
        third = rest - second
        stat = jnp.where(lane_r == g, first, 0.0)
        stat = jnp.where(lane_r == g + 32, second, stat)
        stat = jnp.where(lane_r == g + 64, third, stat)
        msg_f[:, h, :] = norm
        msg_f[:, heads + h, :] = stat
    for r in range(grp_count):
        msg[r] = msg_f[r].astype(BF16)
    got[g] = msg[g]
    for i in order:
        pltpu.make_async_remote_copy(
            msg.at[grp_peer(i)],
            got.at[g],
            send_sems.at[1],
            recv_sems.at[1],
            device_id={"grp": grp_peer(i)},
            device_id_type=MESH,
        ).start()

    new_score = scale * jnp.sum(
        q_all[g].astype(F32) * nk[...].astype(F32), axis=1, keepdims=True
    )
    others = got.at[pl.ds(0, grp_count - 1)]
    pltpu.make_async_copy(others, others, recv_sems.at[1]).wait()

    stat = got[0, heads:, :].astype(F32)
    for r in range(1, grp_count):
        stat = stat + got[r, heads:, :].astype(F32)
    lse = stat + pltpu.roll(stat, 96, 1) + pltpu.roll(stat, 64, 1)
    lse = jnp.where(lane < grp_count, lse, NEG)
    top = jnp.maximum(jnp.max(lse, axis=1, keepdims=True), new_score)
    share = jnp.exp2(lse - top)
    own = jnp.exp2(new_score - top)
    total = jnp.sum(share, axis=1, keepdims=True) + own
    summed = own * nv[...].astype(F32)
    for r in range(grp_count):
        summed = summed + share[:, r : r + 1] * got[r, :heads, :].astype(F32)
    att[g] = (summed / total).astype(BF16)

    for i in order:
        pltpu.make_async_remote_copy(
            att.at[g],
            att.at[g],
            send_sems.at[2],
            recv_sems.at[2],
            device_id={"grp": grp_peer(i)},
            device_id_type=MESH,
        ).start()
    big[2].wait()
    others = att.at[pl.ds(0, grp_count - 1)]
    pltpu.make_async_copy(others, others, recv_sems.at[2]).wait()

    for r in range(grp_count):
        att_f[r] = att[r].astype(F32)
    flat = jnp.concatenate([att_f[:, h, :] for h in range(heads)], axis=1).astype(BF16)
    part = jnp.dot(flat, w[...], preferred_element_type=F32)

    rows = grp_count // 8
    width = part.shape[1] // tp_count
    for p in range(tp_count):
        at = p * width
        tile = jnp.zeros((8, 128), F32)
        for j in range(rows):
            piece = part[8 * j : 8 * j + 8, at // 128 * 128 : at // 128 * 128 + 128]
            shift = (width * j - at) % 128
            if shift:
                piece = pltpu.roll(piece, shift, 1)
            tile = jnp.where(lane // width == j, piece, tile)
        part_out[p] = tile
    part_in[t] = part_out[t]
    for i in tp_order:
        pltpu.make_async_remote_copy(
            part_out.at[tp_peer(i)],
            part_in.at[t],
            send_sems.at[3],
            recv_sems.at[3],
            device_id={"tp": tp_peer(i)},
            device_id_type=MESH,
        ).start()
    others = part_in.at[pl.ds(0, tp_count - 1)]
    pltpu.make_async_copy(others, others, recv_sems.at[3]).wait()
    tile = part_in[0]
    for p in range(1, tp_count):
        tile = tile + part_in[p]
    out_ref[...] = jnp.concatenate(
        [tile[:, width * j : width * (j + 1)] for j in range(rows)], axis=0
    ).astype(BF16)

    for k, ref in enumerate((q_all, got, att)):
        others = ref.at[pl.ds(0, grp_count - 1)]
        pltpu.make_async_copy(others, others, send_sems.at[k]).wait()
    others = part_out.at[pl.ds(0, tp_count - 1)]
    pltpu.make_async_copy(others, others, send_sems.at[3]).wait()


def body(
    queries, new_keys, new_values, key_cache, paged_value_cache, lengths, placement, out_weight
):
    grp_count, tp_count = lax.axis_size("grp"), lax.axis_size("tp")
    slots, _, tokens, head = key_cache.shape
    heads = queries.shape[1]
    requests = lengths.shape[0]
    any_space = pl.BlockSpec(memory_space=pl.ANY)
    scalars = pl.BlockSpec(memory_space=pltpu.SMEM)
    return pl.pallas_call(
        functools.partial(kernel, grp_count, tp_count),
        out_shape=jax.ShapeDtypeStruct((requests, out_weight.shape[1] // tp_count), BF16),
        in_specs=[any_space] * 5 + [scalars] * 2 + [any_space],
        out_specs=pl.BlockSpec(memory_space=pltpu.VMEM),
        scratch_shapes=[
            pltpu.VMEM((requests, heads, head), BF16),
            pltpu.VMEM((1, head), BF16),
            pltpu.VMEM((1, head), BF16),
            pltpu.VMEM((slots, tokens, head), BF16),
            pltpu.VMEM((slots, tokens, head), BF16),
            pltpu.VMEM(out_weight.shape, BF16),
            pltpu.VMEM((slots, heads, head), BF16),
            pltpu.VMEM((slots, heads, tokens), F32),
            pltpu.VMEM((requests, heads, head), F32),
            pltpu.VMEM((slots, heads, head), F32),
            pltpu.VMEM((slots, heads, head), F32),
            pltpu.VMEM((requests, 2 * heads, head), F32),
            pltpu.VMEM((requests, 2 * heads, head), BF16),
            pltpu.VMEM((requests, 2 * heads, head), BF16),
            pltpu.VMEM((requests, heads, head), BF16),
            pltpu.VMEM((requests, heads, head), F32),
            pltpu.VMEM((tp_count, 8, 128), F32),
            pltpu.VMEM((tp_count, 8, 128), F32),
            pltpu.SemaphoreType.DMA((3,)),
            pltpu.SemaphoreType.DMA,
            pltpu.SemaphoreType.DMA,
            pltpu.SemaphoreType.DMA,
            pltpu.SemaphoreType.DMA((4,)),
            pltpu.SemaphoreType.DMA((4,)),
        ],
        compiler_params=pltpu.CompilerParams(
            collective_id=0, has_side_effects=True, vmem_limit_bytes=48 << 20
        ),
    )(
        queries,
        new_keys,
        new_values,
        key_cache.reshape(slots, tokens, head),
        paged_value_cache.reshape(slots, tokens, head),
        lengths,
        placement,
        out_weight,
    )


def solution(mesh):
    in_specs = (
        P("grp", "tp", None),
        P("grp", "tp", None),
        P("grp", "tp", None),
        P("grp", "tp", None, None),
        P("grp", "tp", None, None),
        P(),
        P("grp", None),
        P("tp", "grp"),
    )
    out_specs = P(None, ("grp", "tp"))
    return jax.shard_map(body, mesh=mesh, in_specs=in_specs, out_specs=out_specs, check_vma=False)
```

```python
import functools
import math

import jax
import jax.numpy as jnp
from jax import lax
from jax.experimental import pallas as pl
from jax.experimental.pallas import tpu as pltpu
from jax.sharding import PartitionSpec as P

MESH = pl.DeviceIdType.MESH
NEG = -1e30
F32 = jnp.float32
BF16 = jnp.bfloat16


def torus(z_extent, y_extent):
    found = []
    for dz in range(z_extent):
        for dy in range(y_extent):
            far = min(dz, z_extent - dz) + min(dy, y_extent - dy)
            if far:
                found.append((far, dz, dy))
    return sorted(found, key=lambda f: (-f[0], f[1], f[2]))


def tree(terms):
    while len(terms) > 1:
        terms = [a + b for a, b in zip(terms[::2], terms[1::2])] + terms[len(terms) // 2 * 2 :]
    return terms[0]


Z, Y = 8, 4
OFFSETS = torus(Z, Y)
NEAR = [f for f in OFFSETS if f[0] < 3 or f in ((3, 1, 2), (3, 7, 2), (3, 2, 1), (3, 6, 1))]
NEAR = sorted(NEAR, key=lambda f: -f[0])


def kernel(
    grp_count,
    tp_count,
    q_hbm,
    nk_hbm,
    nv_hbm,
    k_hbm,
    v_hbm,
    len_hbm,
    place_hbm,
    w_hbm,
    out_ref,
    q_all,
    nk,
    nv,
    keys,
    keys_t,
    vals,
    w,
    len_ref,
    place_ref,
    scores,
    group_max,
    mix,
    tot,
    norm_f,
    msg,
    got,
    stat_out,
    stat_in,
    att,
    att_f,
    part_out,
    part_in,
    sem_small,
    sem_k,
    sem_v,
    sem_w,
    send_sems,
    recv_sems,
):
    g = lax.axis_index("grp")
    t = lax.axis_index("tp")
    slots, tokens, head = keys.shape
    heads = q_all.shape[1]
    padded = mix.shape[0]
    scale = head**-0.5 * math.log2(math.e)
    gz, gy = g // Y, lax.rem(g, Y)
    tp_order = sorted(range(1, tp_count), key=lambda i: -min(i, tp_count - i))

    def grp_at(dz, dy):
        return lax.rem(gz + dz, Z) * Y + lax.rem(gy + dy, Y)

    def tp_peer(i):
        return lax.rem(t + i, tp_count)

    def push(src, dst, k, device_id):
        pltpu.make_async_remote_copy(
            src,
            dst,
            send_sems.at[k],
            recv_sems.at[k],
            device_id=device_id,
            device_id_type=MESH,
        ).start()

    def await_bytes(ref, count, sem):
        some = ref.at[pl.ds(0, count)]
        pltpu.make_async_copy(some, some, sem).wait()

    barrier = pltpu.get_barrier_semaphore()
    for _, dz, dy in OFFSETS:
        pl.semaphore_signal(barrier, 1, device_id={"grp": grp_at(dz, dy)}, device_id_type=MESH)
    for i in tp_order:
        pl.semaphore_signal(barrier, 1, device_id={"tp": tp_peer(i)}, device_id_type=MESH)

    small = [
        pltpu.make_async_copy(q_hbm.at[0], q_all.at[g], sem_small.at[0]),
        pltpu.make_async_copy(nk_hbm.at[0], nk, sem_small.at[1]),
        pltpu.make_async_copy(nv_hbm.at[0], nv, sem_small.at[2]),
        pltpu.make_async_copy(len_hbm, len_ref, sem_small.at[3]),
        pltpu.make_async_copy(place_hbm, place_ref, sem_small.at[4]),
    ]
    for c in small:
        c.start()
    big = [
        pltpu.make_async_copy(k_hbm, keys, sem_k),
        pltpu.make_async_copy(v_hbm, vals, sem_v),
        pltpu.make_async_copy(w_hbm, w, sem_w),
    ]
    for c in big:
        c.start()
    for c in small:
        c.wait()

    pl.semaphore_wait(barrier, grp_count - 1 + tp_count - 1)
    for _, dz, dy in OFFSETS:
        push(q_all.at[g], q_all.at[g], 0, {"grp": grp_at(dz, dy)})

    lane = lax.broadcasted_iota(jnp.int32, (heads, 128), 1)
    row = lax.broadcasted_iota(jnp.int32, (grp_count, 128), 0)
    lane_r = lax.broadcasted_iota(jnp.int32, (grp_count, 128), 1)
    token = lax.broadcasted_iota(jnp.int32, (heads, tokens), 1)

    owner_row = jnp.where(lane == slots, g, grp_count)
    for s in range(slots):
        owner_row = jnp.where(lane == s, place_ref[0, s], owner_row)
    onehot = jnp.where(owner_row[:1, :] == row, 1.0, 0.0)[:, :padded].astype(BF16)
    onehot2 = jnp.concatenate([onehot, onehot], axis=1)
    for s in range(slots, padded):
        mix[s] = jnp.zeros((heads, head), F32)
        tot[s] = jnp.zeros((heads, head), F32)
    new_score = scale * jnp.sum(
        q_all[g].astype(F32) * nk[...].astype(F32), axis=1, keepdims=True
    )
    new_score = jnp.broadcast_to(new_score, (heads, 128))
    big[0].wait()
    for s in range(slots):
        keys_t[s] = keys[s].T
    await_bytes(q_all, grp_count - 1, recv_sems.at[0])

    slot_max = jnp.where(lane == slots, new_score, NEG)
    for s in range(slots):
        owner = place_ref[0, s]
        request = jnp.minimum(owner, grp_count - 1)
        live = jnp.where(owner < grp_count, len_ref[request] - place_ref[1, s] * tokens, 0)
        x = jnp.dot(q_all[request], keys_t[s], preferred_element_type=F32)
        x = jnp.where(token < live, x * scale, NEG)
        scores[s] = x
        slot_max = jnp.where(lane == s, jnp.max(x, axis=1, keepdims=True), slot_max)
    for r in range(grp_count):
        top = jnp.max(jnp.where(owner_row == r, slot_max, NEG), axis=1, keepdims=True)
        group_max[r] = jnp.broadcast_to(top, (heads, 128))

    weight = jnp.exp2(new_score - group_max[g])
    mix[slots] = weight * nv[...].astype(F32)
    tot[slots] = weight
    big[1].wait()
    for s in range(slots):
        top = group_max[jnp.minimum(place_ref[0, s], grp_count - 1)]
        p = jnp.exp2(scores[s] - jnp.concatenate([top, top], axis=1))
        mix[s] = jnp.dot(p.astype(BF16), vals[s], preferred_element_type=F32)
        tot[s] = jnp.broadcast_to(jnp.sum(p, axis=1, keepdims=True), (heads, head))

    stat = jnp.full((grp_count, 128), NEG, F32)
    for h in range(heads):
        both = jnp.concatenate([mix[:, h, :], tot[:, h, :]], axis=1)
        hi = both.astype(BF16)
        lo = (both - hi.astype(F32)).astype(BF16)
        sums = jnp.dot(onehot2, jnp.concatenate([hi, lo], axis=0), preferred_element_type=F32)
        value_sum, weight_sum = sums[:, :128], sums[:, 128:]
        there = weight_sum > 0.0
        safe = jnp.where(there, weight_sum, 1.0)
        norm_f[:, h, :] = value_sum / safe
        lse = jnp.where(there, group_max[:, h, :] + jnp.log2(safe), NEG)
        stat = jnp.where(lane_r == h, lse, stat)
    other = jnp.concatenate([stat[grp_count // 2 :], stat[: grp_count // 2]], axis=0)
    other = jnp.where(
        lax.rem(row, 4) < 2, pltpu.roll(other, grp_count - 2, 0), pltpu.roll(other, 2, 0)
    )
    stat = jnp.where((lane_r >= heads) & (lane_r < 2 * heads), pltpu.roll(other, heads, 1), stat)
    stat_out[:, 0, :] = stat
    for r in range(grp_count):
        msg[r] = jnp.concatenate([norm_f[r], norm_f[r ^ 18]], axis=0).astype(BF16)
    got[g] = msg[g]
    stat_in[g] = stat_out[g]
    for _, dz, dy in OFFSETS:
        p = grp_at(dz, dy)
        push(msg.at[p], got.at[g], 1, {"grp": p})
        push(stat_out.at[p], stat_in.at[g], 2, {"grp": p})
    await_bytes(stat_in, grp_count - 1, recv_sems.at[2])
    await_bytes(got, grp_count - 1, recv_sems.at[1])

    lse = stat_in[:, 0, :]
    share = jnp.exp2(lse - jnp.max(lse, axis=0, keepdims=True))
    share = share / jnp.sum(share, axis=0, keepdims=True)
    share = share.T[: 2 * heads, :]
    att[g] = tree(
        [share[:, r : r + 1] * got[r].astype(F32) for r in range(grp_count)]
    ).astype(BF16)

    for _, dz, dy in NEAR:
        push(att.at[g], att.at[g], 3, {"grp": grp_at(dz, dy)})
    big[2].wait()
    await_bytes(att, len(NEAR), recv_sems.at[3])

    for dz, dy in [(0, 0)] + [(dz, dy) for _, dz, dy in NEAR]:
        home = grp_at(Z - dz, Y - dy)
        both = att[home].astype(F32)
        att_f[home] = both[:heads]
        att_f[grp_at(Z - dz + Z // 2, Y - dy + Y // 2)] = both[heads:]
    flat = jnp.concatenate([att_f[:, h, :] for h in range(heads)], axis=1).astype(BF16)
    part = jnp.dot(flat, w[...], preferred_element_type=F32)

    rows = grp_count // 8
    width = part.shape[1] // tp_count
    for p in range(tp_count):
        at = p * width
        tile = jnp.zeros((8, 128), F32)
        for j in range(rows):
            piece = part[8 * j : 8 * j + 8, at // 128 * 128 : at // 128 * 128 + 128]
            shift = (width * j - at) % 128
            if shift:
                piece = pltpu.roll(piece, shift, 1)
            tile = jnp.where(lane // width == j, piece, tile)
        part_out[p] = tile
    part_in[t] = part_out[t]
    for i in tp_order:
        push(part_out.at[tp_peer(i)], part_in.at[t], 4, {"tp": tp_peer(i)})
    await_bytes(part_in, tp_count - 1, recv_sems.at[4])
    tile = tree([part_in[p] for p in range(tp_count)])
    out_ref[...] = jnp.concatenate(
        [tile[:, width * j : width * (j + 1)] for j in range(rows)], axis=0
    ).astype(BF16)

    await_bytes(q_all, grp_count - 1, send_sems.at[0])
    await_bytes(msg, grp_count - 1, send_sems.at[1])
    await_bytes(stat_out, grp_count - 1, send_sems.at[2])
    await_bytes(att, len(NEAR), send_sems.at[3])
    await_bytes(part_out, tp_count - 1, send_sems.at[4])


def body(
    queries, new_keys, new_values, key_cache, paged_value_cache, lengths, placement, out_weight
):
    grp_count, tp_count = lax.axis_size("grp"), lax.axis_size("tp")
    slots, _, tokens, head = key_cache.shape
    heads = queries.shape[1]
    requests = lengths.shape[0]
    padded = slots + 16
    return pl.pallas_call(
        functools.partial(kernel, grp_count, tp_count),
        out_shape=jax.ShapeDtypeStruct((requests, out_weight.shape[1] // tp_count), BF16),
        in_specs=[pl.BlockSpec(memory_space=pltpu.HBM)] * 8,
        out_specs=pl.BlockSpec(memory_space=pltpu.VMEM),
        scratch_shapes=[
            pltpu.VMEM((requests, heads, head), BF16),
            pltpu.VMEM((1, head), BF16),
            pltpu.VMEM((1, head), BF16),
            pltpu.VMEM((slots, tokens, head), BF16),
            pltpu.VMEM((slots, head, tokens), BF16),
            pltpu.VMEM((slots, tokens, head), BF16),
            pltpu.VMEM(out_weight.shape, BF16),
            pltpu.SMEM(lengths.shape, jnp.int32),
            pltpu.SMEM((2, slots), jnp.int32),
            pltpu.VMEM((slots, heads, tokens), F32),
            pltpu.VMEM((requests, heads, head), F32),
            pltpu.VMEM((padded, heads, head), F32),
            pltpu.VMEM((padded, heads, head), F32),
            pltpu.VMEM((requests, heads, head), F32),
            pltpu.VMEM((requests, 2 * heads, head), BF16),
            pltpu.VMEM((requests, 2 * heads, head), BF16),
            pltpu.VMEM((requests, 1, 128), F32),
            pltpu.VMEM((requests, 1, 128), F32),
            pltpu.VMEM((requests, 2 * heads, head), BF16),
            pltpu.VMEM((requests, heads, head), F32),
            pltpu.VMEM((tp_count, 8, 128), F32),
            pltpu.VMEM((tp_count, 8, 128), F32),
            pltpu.SemaphoreType.DMA((5,)),
            pltpu.SemaphoreType.DMA,
            pltpu.SemaphoreType.DMA,
            pltpu.SemaphoreType.DMA,
            pltpu.SemaphoreType.DMA((5,)),
            pltpu.SemaphoreType.DMA((5,)),
        ],
        compiler_params=pltpu.CompilerParams(
            collective_id=0, has_side_effects=True, vmem_limit_bytes=56 << 20
        ),
    )(
        queries,
        new_keys,
        new_values,
        key_cache.reshape(slots, tokens, head),
        paged_value_cache.reshape(slots, tokens, head),
        lengths,
        placement.T,
        out_weight,
    )


def solution(mesh):
    in_specs = (
        P("grp", "tp", None),
        P("grp", "tp", None),
        P("grp", "tp", None),
        P("grp", "tp", None, None),
        P("grp", "tp", None, None),
        P(),
        P("grp", None),
        P("tp", "grp"),
    )
    out_specs = P(None, ("grp", "tp"))
    return jax.shard_map(body, mesh=mesh, in_specs=in_specs, out_specs=out_specs, check_vma=False)
```

```python
import functools
import math

import jax
import jax.numpy as jnp
from jax import lax
from jax.experimental import pallas as pl
from jax.experimental.pallas import tpu as pltpu
from jax.sharding import PartitionSpec as P

MESH = pl.DeviceIdType.MESH
NEG = -1e30
F32 = jnp.float32
BF16 = jnp.bfloat16


def torus(z_extent, y_extent):
    found = []
    for dz in range(z_extent):
        for dy in range(y_extent):
            far = min(dz, z_extent - dz) + min(dy, y_extent - dy)
            if far:
                found.append((far, dz, dy))
    return sorted(found, key=lambda f: (-f[0], f[1], f[2]))


def tree(terms):
    while len(terms) > 1:
        terms = [a + b for a, b in zip(terms[::2], terms[1::2])] + terms[len(terms) // 2 * 2 :]
    return terms[0]


Z, Y = 8, 4
OFFSETS = torus(Z, Y)
NEAR = [f for f in OFFSETS if f[0] < 3 or f in ((3, 1, 2), (3, 7, 2), (3, 2, 1), (3, 6, 1))]
NEAR = sorted(NEAR, key=lambda f: -f[0])


def kernel(
    grp_count,
    tp_count,
    q_hbm,
    nk_hbm,
    nv_hbm,
    k_hbm,
    v_hbm,
    len_hbm,
    place_hbm,
    w_hbm,
    out_ref,
    q_all,
    nk,
    nv,
    keys,
    keys_t,
    vals,
    w,
    len_ref,
    place_ref,
    scores,
    group_max,
    mix,
    tot,
    norm_f,
    msg,
    got,
    stat_out,
    stat_in,
    att,
    att_f,
    part_out,
    part_in,
    sem_small,
    sem_k,
    sem_v,
    sem_w,
    send_sems,
    recv_sems,
):
    g = lax.axis_index("grp")
    t = lax.axis_index("tp")
    slots, tokens, head = keys.shape
    heads = q_all.shape[1]
    padded = mix.shape[0]
    scale = head**-0.5 * math.log2(math.e)
    gz, gy = g // Y, lax.rem(g, Y)
    tp_order = sorted(range(1, tp_count), key=lambda i: -min(i, tp_count - i))

    def grp_at(dz, dy):
        return lax.rem(gz + dz, Z) * Y + lax.rem(gy + dy, Y)

    def tp_peer(i):
        return lax.rem(t + i, tp_count)

    def push(src, dst, k, device_id):
        pltpu.make_async_remote_copy(
            src,
            dst,
            send_sems.at[k],
            recv_sems.at[k],
            device_id=device_id,
            device_id_type=MESH,
        ).start()

    def await_bytes(ref, count, sem):
        some = ref.at[pl.ds(0, count)]
        pltpu.make_async_copy(some, some, sem).wait()

    barrier = pltpu.get_barrier_semaphore()
    for _, dz, dy in OFFSETS:
        pl.semaphore_signal(barrier, 1, device_id={"grp": grp_at(dz, dy)}, device_id_type=MESH)
    for i in tp_order:
        pl.semaphore_signal(barrier, 1, device_id={"tp": tp_peer(i)}, device_id_type=MESH)

    small = [
        pltpu.make_async_copy(q_hbm.at[0], q_all.at[g], sem_small.at[0]),
        pltpu.make_async_copy(nk_hbm.at[0], nk, sem_small.at[1]),
        pltpu.make_async_copy(nv_hbm.at[0], nv, sem_small.at[2]),
        pltpu.make_async_copy(len_hbm, len_ref, sem_small.at[3]),
        pltpu.make_async_copy(place_hbm, place_ref, sem_small.at[4]),
    ]
    for c in small:
        c.start()
    big = [
        pltpu.make_async_copy(k_hbm, keys, sem_k),
        pltpu.make_async_copy(v_hbm, vals, sem_v),
        pltpu.make_async_copy(w_hbm, w, sem_w),
    ]
    for c in big:
        c.start()
    for c in small:
        c.wait()

    pl.semaphore_wait(barrier, grp_count - 1 + tp_count - 1)
    for _, dz, dy in OFFSETS:
        push(q_all.at[g], q_all.at[g], 0, {"grp": grp_at(dz, dy)})

    lane = lax.broadcasted_iota(jnp.int32, (heads, 128), 1)
    row = lax.broadcasted_iota(jnp.int32, (grp_count, 128), 0)
    lane_r = lax.broadcasted_iota(jnp.int32, (grp_count, 128), 1)
    token = lax.broadcasted_iota(jnp.int32, (heads, tokens), 1)

    owner_row = jnp.where(lane == slots, g, grp_count)
    for s in range(slots):
        owner_row = jnp.where(lane == s, place_ref[0, s], owner_row)
    onehot = jnp.where(owner_row[:1, :] == row, 1.0, 0.0)[:, :padded].astype(BF16)
    onehot2 = jnp.concatenate([onehot, onehot], axis=1)
    for s in range(slots, padded):
        mix[s] = jnp.zeros((heads, head), F32)
        tot[s] = jnp.zeros((heads, head), F32)
    new_score = scale * jnp.sum(
        q_all[g].astype(F32) * nk[...].astype(F32), axis=1, keepdims=True
    )
    new_score = jnp.broadcast_to(new_score, (heads, 128))
    big[0].wait()
    for s in range(slots):
        keys_t[s] = keys[s].T
    await_bytes(q_all, grp_count - 1, recv_sems.at[0])

    slot_max = jnp.where(lane == slots, new_score, NEG)
    for s in range(slots):
        owner = place_ref[0, s]
        request = jnp.minimum(owner, grp_count - 1)
        live = jnp.where(owner < grp_count, len_ref[request] - place_ref[1, s] * tokens, 0)
        x = jnp.dot(q_all[request], keys_t[s], preferred_element_type=F32)
        x = jnp.where(token < live, x * scale, NEG)
        scores[s] = x
        slot_max = jnp.where(lane == s, jnp.max(x, axis=1, keepdims=True), slot_max)
    for r in range(grp_count):
        top = jnp.max(jnp.where(owner_row == r, slot_max, NEG), axis=1, keepdims=True)
        group_max[r] = jnp.broadcast_to(top, (heads, 128))

    weight = jnp.exp2(new_score - group_max[g])
    mix[slots] = weight * nv[...].astype(F32)
    tot[slots] = weight
    big[1].wait()
    for s in range(slots):
        top = group_max[jnp.minimum(place_ref[0, s], grp_count - 1)]
        p = jnp.exp2(scores[s] - jnp.concatenate([top, top], axis=1))
        mix[s] = jnp.dot(p.astype(BF16), vals[s], preferred_element_type=F32)
        tot[s] = jnp.broadcast_to(jnp.sum(p, axis=1, keepdims=True), (heads, head))

    stat = jnp.full((grp_count, 128), NEG, F32)
    for h in range(heads):
        both = jnp.concatenate([mix[:, h, :], tot[:, h, :]], axis=1)
        hi = both.astype(BF16)
        lo = (both - hi.astype(F32)).astype(BF16)
        sums = jnp.dot(onehot2, jnp.concatenate([hi, lo], axis=0), preferred_element_type=F32)
        value_sum, weight_sum = sums[:, :128], sums[:, 128:]
        there = weight_sum > 0.0
        safe = jnp.where(there, weight_sum, 1.0)
        norm_f[:, h, :] = value_sum / safe
        lse = jnp.where(there, group_max[:, h, :] + jnp.log2(safe), NEG)
        stat = jnp.where(lane_r == h, lse, stat)
    other = jnp.concatenate([stat[grp_count // 2 :], stat[: grp_count // 2]], axis=0)
    other = jnp.where(
        lax.rem(row, 4) < 2, pltpu.roll(other, grp_count - 2, 0), pltpu.roll(other, 2, 0)
    )
    stat = jnp.where((lane_r >= heads) & (lane_r < 2 * heads), pltpu.roll(other, heads, 1), stat)
    stat_out[:, 0, :] = stat
    for r in range(grp_count):
        msg[r] = jnp.concatenate([norm_f[r], norm_f[r ^ 18]], axis=0).astype(BF16)
    got[g] = msg[g]
    stat_in[g] = stat_out[g]
    for _, dz, dy in OFFSETS:
        p = grp_at(dz, dy)
        push(msg.at[p], got.at[g], 1, {"grp": p})
        push(stat_out.at[p], stat_in.at[g], 2, {"grp": p})
    await_bytes(stat_in, grp_count - 1, recv_sems.at[2])
    await_bytes(got, grp_count - 1, recv_sems.at[1])

    lse = stat_in[:, 0, :]
    share = jnp.exp2(lse - jnp.max(lse, axis=0, keepdims=True))
    share = share / jnp.sum(share, axis=0, keepdims=True)
    share = share.T[: 2 * heads, :]
    att[g] = tree(
        [share[:, r : r + 1] * got[r].astype(F32) for r in range(grp_count)]
    ).astype(BF16)

    for _, dz, dy in NEAR:
        push(att.at[g], att.at[g], 3, {"grp": grp_at(dz, dy)})
    big[2].wait()
    await_bytes(att, len(NEAR), recv_sems.at[3])

    for dz, dy in [(0, 0)] + [(dz, dy) for _, dz, dy in NEAR]:
        home = grp_at(Z - dz, Y - dy)
        both = att[home].astype(F32)
        att_f[home] = both[:heads]
        att_f[grp_at(Z - dz + Z // 2, Y - dy + Y // 2)] = both[heads:]
    flat = jnp.concatenate([att_f[:, h, :] for h in range(heads)], axis=1).astype(BF16)
    part = jnp.dot(flat, w[...], preferred_element_type=F32)

    rows = grp_count // 8
    width = part.shape[1] // tp_count
    for p in range(tp_count):
        at = p * width
        tile = jnp.zeros((8, 128), F32)
        for j in range(rows):
            piece = part[8 * j : 8 * j + 8, at // 128 * 128 : at // 128 * 128 + 128]
            shift = (width * j - at) % 128
            if shift:
                piece = pltpu.roll(piece, shift, 1)
            tile = jnp.where(lane // width == j, piece, tile)
        part_out[p] = tile
    part_in[t] = part_out[t]
    for i in tp_order:
        push(part_out.at[tp_peer(i)], part_in.at[t], 4, {"tp": tp_peer(i)})
    await_bytes(part_in, tp_count - 1, recv_sems.at[4])
    tile = tree([part_in[p] for p in range(tp_count)])
    out_ref[...] = jnp.concatenate(
        [tile[:, width * j : width * (j + 1)] for j in range(rows)], axis=0
    ).astype(BF16)

    await_bytes(q_all, grp_count - 1, send_sems.at[0])
    await_bytes(msg, grp_count - 1, send_sems.at[1])
    await_bytes(stat_out, grp_count - 1, send_sems.at[2])
    await_bytes(att, len(NEAR), send_sems.at[3])
    await_bytes(part_out, tp_count - 1, send_sems.at[4])


def body(
    queries, new_keys, new_values, key_cache, paged_value_cache, lengths, placement, out_weight
):
    grp_count, tp_count = lax.axis_size("grp"), lax.axis_size("tp")
    slots, _, tokens, head = key_cache.shape
    heads = queries.shape[1]
    requests = lengths.shape[0]
    padded = slots + 16
    return pl.pallas_call(
        functools.partial(kernel, grp_count, tp_count),
        out_shape=pltpu.VMEM((requests, out_weight.shape[1] // tp_count), BF16),
        in_specs=[pl.BlockSpec(memory_space=pltpu.HBM)] * 8,
        out_specs=pl.BlockSpec(memory_space=pltpu.VMEM),
        scratch_shapes=[
            pltpu.VMEM((requests, heads, head), BF16),
            pltpu.VMEM((1, head), BF16),
            pltpu.VMEM((1, head), BF16),
            pltpu.VMEM((slots, tokens, head), BF16),
            pltpu.VMEM((slots, head, tokens), BF16),
            pltpu.VMEM((slots, tokens, head), BF16),
            pltpu.VMEM(out_weight.shape, BF16),
            pltpu.SMEM(lengths.shape, jnp.int32),
            pltpu.SMEM((2, slots), jnp.int32),
            pltpu.VMEM((slots, heads, tokens), F32),
            pltpu.VMEM((requests, heads, head), F32),
            pltpu.VMEM((padded, heads, head), F32),
            pltpu.VMEM((padded, heads, head), F32),
            pltpu.VMEM((requests, heads, head), F32),
            pltpu.VMEM((requests, 2 * heads, head), BF16),
            pltpu.VMEM((requests, 2 * heads, head), BF16),
            pltpu.VMEM((requests, 1, 128), F32),
            pltpu.VMEM((requests, 1, 128), F32),
            pltpu.VMEM((requests, 2 * heads, head), BF16),
            pltpu.VMEM((requests, heads, head), F32),
            pltpu.VMEM((tp_count, 8, 128), F32),
            pltpu.VMEM((tp_count, 8, 128), F32),
            pltpu.SemaphoreType.DMA((5,)),
            pltpu.SemaphoreType.DMA,
            pltpu.SemaphoreType.DMA,
            pltpu.SemaphoreType.DMA,
            pltpu.SemaphoreType.DMA((5,)),
            pltpu.SemaphoreType.DMA((5,)),
        ],
        compiler_params=pltpu.CompilerParams(
            collective_id=0, has_side_effects=True, vmem_limit_bytes=32 << 20
        ),
    )(
        *(
            pltpu.with_memory_space_constraint(x, pltpu.HBM)
            for x in (
                queries,
                new_keys,
                new_values,
                key_cache.reshape(slots, tokens, head),
                paged_value_cache.reshape(slots, tokens, head),
                lengths,
                placement.T,
                out_weight,
            )
        )
    )


def solution(mesh):
    in_specs = (
        P("grp", "tp", None),
        P("grp", "tp", None),
        P("grp", "tp", None),
        P("grp", "tp", None, None),
        P("grp", "tp", None, None),
        P(),
        P("grp", None),
        P("tp", "grp"),
    )
    out_specs = P(None, ("grp", "tp"))
    return jax.shard_map(body, mesh=mesh, in_specs=in_specs, out_specs=out_specs, check_vma=False)
```

```python
import functools
import math

import jax
import jax.numpy as jnp
from jax import lax
from jax.experimental import pallas as pl
from jax.experimental.pallas import tpu as pltpu
from jax.sharding import PartitionSpec as P

MESH = pl.DeviceIdType.MESH
NEG = -1e30
F32 = jnp.float32
BF16 = jnp.bfloat16


def torus(z_extent, y_extent):
    found = []
    for dz in range(z_extent):
        for dy in range(y_extent):
            far = min(dz, z_extent - dz) + min(dy, y_extent - dy)
            if far:
                found.append((far, dz, dy))
    return sorted(found, key=lambda f: (-f[0], f[1], f[2]))


def tree(terms):
    while len(terms) > 1:
        terms = [a + b for a, b in zip(terms[::2], terms[1::2])] + terms[len(terms) // 2 * 2 :]
    return terms[0]


Z, Y = 8, 4
OFFSETS = torus(Z, Y)
NEAR = [f for f in OFFSETS if f[0] < 3 or f in ((3, 5, 0), (3, 3, 0), (3, 2, 1), (3, 6, 1))]
NEAR = sorted(NEAR, key=lambda f: -f[0])


def kernel(
    grp_count,
    tp_count,
    q_hbm,
    nk_hbm,
    nv_hbm,
    k_hbm,
    v_hbm,
    len_hbm,
    place_hbm,
    w_hbm,
    out_ref,
    q_all,
    nk,
    nv,
    keys,
    keys_t,
    vals,
    w,
    len_ref,
    place_ref,
    scores,
    group_max,
    mix,
    tot,
    norm_f,
    adder,
    msg,
    got,
    stat_out,
    stat_in,
    att,
    att_f,
    part_out,
    part_in,
    sem_small,
    sem_k,
    sem_v,
    sem_w,
    send_sems,
    recv_sems,
):
    g = lax.axis_index("grp")
    t = lax.axis_index("tp")
    slots, tokens, head = keys.shape
    heads = q_all.shape[1]
    padded = mix.shape[0]
    scale = head**-0.5 * math.log2(math.e)
    gz, gy = g // Y, lax.rem(g, Y)
    tp_order = sorted(range(1, tp_count), key=lambda i: -min(i, tp_count - i))

    def grp_at(dz, dy):
        return lax.rem(gz + dz, Z) * Y + lax.rem(gy + dy, Y)

    def tp_peer(i):
        return lax.rem(t + i, tp_count)

    def push(src, dst, k, device_id):
        pltpu.make_async_remote_copy(
            src,
            dst,
            send_sems.at[k],
            recv_sems.at[k],
            device_id=device_id,
            device_id_type=MESH,
        ).start()

    def await_bytes(ref, count, sem):
        some = ref.at[pl.ds(0, count)]
        pltpu.make_async_copy(some, some, sem).wait()

    barrier = pltpu.get_barrier_semaphore()
    for _, dz, dy in OFFSETS:
        pl.semaphore_signal(barrier, 1, device_id={"grp": grp_at(dz, dy)}, device_id_type=MESH)
    for i in tp_order:
        pl.semaphore_signal(barrier, 1, device_id={"tp": tp_peer(i)}, device_id_type=MESH)

    small = [
        pltpu.make_async_copy(q_hbm.at[0], q_all.at[g], sem_small.at[0]),
        pltpu.make_async_copy(nk_hbm.at[0], nk, sem_small.at[1]),
        pltpu.make_async_copy(nv_hbm.at[0], nv, sem_small.at[2]),
        pltpu.make_async_copy(len_hbm, len_ref, sem_small.at[3]),
        pltpu.make_async_copy(place_hbm, place_ref, sem_small.at[4]),
    ]
    for c in small:
        c.start()
    big = [
        pltpu.make_async_copy(k_hbm, keys, sem_k),
        pltpu.make_async_copy(v_hbm, vals, sem_v),
        pltpu.make_async_copy(w_hbm, w, sem_w),
    ]
    for c in big:
        c.start()
    for c in small:
        c.wait()

    pl.semaphore_wait(barrier, grp_count - 1 + tp_count - 1)
    for _, dz, dy in OFFSETS:
        push(q_all.at[g], q_all.at[g], 0, {"grp": grp_at(dz, dy)})

    lane = lax.broadcasted_iota(jnp.int32, (heads, 128), 1)
    row = lax.broadcasted_iota(jnp.int32, (grp_count, 128), 0)
    lane_r = lax.broadcasted_iota(jnp.int32, (grp_count, 128), 1)
    token = lax.broadcasted_iota(jnp.int32, (heads, tokens), 1)

    owner_row = jnp.where(lane == slots, g, grp_count)
    for s in range(slots):
        owner_row = jnp.where(lane == s, place_ref[0, s], owner_row)
    per_tile = 128 // heads
    big_row = lax.broadcasted_iota(jnp.int32, (grp_count * heads, 128), 0)
    big_lane = lax.broadcasted_iota(jnp.int32, (grp_count * heads, 128), 1)
    same_head = lax.rem(big_row, heads) == lax.rem(big_lane, heads)
    for c in range(padded // per_tile):
        owners = jnp.full((1, 128), grp_count, jnp.int32)
        if c * per_tile == slots:
            owners = jnp.where(lane[:1] < heads, g, grp_count)
        for s in range(c * per_tile, min(slots, (c + 1) * per_tile)):
            owners = jnp.where(lane[:1] // heads == s - c * per_tile, place_ref[0, s], owners)
        block = jnp.where(same_head & (owners == big_row // heads), 1.0, 0.0)
        adder[:, c * 128 : (c + 1) * 128] = block.astype(BF16)
    for s in range(slots, padded):
        mix[s] = jnp.zeros((heads, head), F32)
        tot[s] = jnp.zeros((heads, head), F32)
    new_score = scale * jnp.sum(
        q_all[g].astype(F32) * nk[...].astype(F32), axis=1, keepdims=True
    )
    new_score = jnp.broadcast_to(new_score, (heads, 128))
    big[0].wait()
    for s in range(slots):
        keys_t[s] = keys[s].T
    await_bytes(q_all, grp_count - 1, recv_sems.at[0])

    slot_max = jnp.where(lane == slots, new_score, NEG)
    for s in range(slots):
        owner = place_ref[0, s]
        request = jnp.minimum(owner, grp_count - 1)
        live = jnp.where(owner < grp_count, len_ref[request] - place_ref[1, s] * tokens, 0)
        x = jnp.dot(q_all[request], keys_t[s], preferred_element_type=F32)
        x = jnp.where(token < live, x * scale, NEG)
        scores[s] = x
        slot_max = jnp.where(lane == s, jnp.max(x, axis=1, keepdims=True), slot_max)
    for r in range(grp_count):
        top = jnp.max(jnp.where(owner_row == r, slot_max, NEG), axis=1, keepdims=True)
        group_max[r] = jnp.broadcast_to(top, (heads, 128))

    weight = jnp.exp2(new_score - group_max[g])
    mix[slots] = weight * nv[...].astype(F32)
    tot[slots] = weight
    big[1].wait()
    for s in range(slots):
        top = group_max[jnp.minimum(place_ref[0, s], grp_count - 1)]
        p = jnp.exp2(scores[s] - jnp.concatenate([top, top], axis=1))
        mix[s] = jnp.dot(p.astype(BF16), vals[s], preferred_element_type=F32)
        tot[s] = jnp.broadcast_to(jnp.sum(p, axis=1, keepdims=True), (heads, head))

    both = jnp.concatenate(
        [mix[...].reshape(padded * heads, head), tot[...].reshape(padded * heads, head)], axis=1
    )
    hi = both.astype(BF16)
    lo = (both - hi.astype(F32)).astype(BF16)
    sums = jnp.dot(adder[...], hi, preferred_element_type=F32)
    sums = sums + jnp.dot(adder[...], lo, preferred_element_type=F32)
    value_sum, weight_sum = sums[:, :128], sums[:, 128:]
    there = weight_sum > 0.0
    safe = jnp.where(there, weight_sum, 1.0)
    norm = (value_sum / safe).reshape(grp_count, heads, head)
    lse = jnp.where(there, group_max[...].reshape(grp_count * heads, 128) + jnp.log2(safe), NEG)
    norm_f[...] = lse.reshape(grp_count, heads, head)
    stat = jnp.full((grp_count, 128), NEG, F32)
    for h in range(heads):
        stat = jnp.where(lane_r == h, norm_f[:, h, :], stat)
    other = jnp.concatenate([stat[grp_count // 2 :], stat[: grp_count // 2]], axis=0)
    other = jnp.where(
        lax.rem(row, 4) < 2, pltpu.roll(other, grp_count - 2, 0), pltpu.roll(other, 2, 0)
    )
    stat = jnp.where((lane_r >= heads) & (lane_r < 2 * heads), pltpu.roll(other, heads, 1), stat)
    stat_out[:, 0, :] = stat
    for r in range(grp_count):
        msg[r] = jnp.concatenate([norm[r], norm[r ^ 18]], axis=0).astype(BF16)
    got[g] = msg[g]
    stat_in[g] = stat_out[g]
    for _, dz, dy in OFFSETS:
        p = grp_at(dz, dy)
        push(msg.at[p], got.at[g], 1, {"grp": p})
        push(stat_out.at[p], stat_in.at[g], 2, {"grp": p})
    await_bytes(stat_in, grp_count - 1, recv_sems.at[2])
    await_bytes(got, grp_count - 1, recv_sems.at[1])

    lse = stat_in[:, 0, :]
    share = jnp.exp2(lse - jnp.max(lse, axis=0, keepdims=True))
    share = share / jnp.sum(share, axis=0, keepdims=True)
    share = share.T[: 2 * heads, :]
    att[g] = tree(
        [share[:, r : r + 1] * got[r].astype(F32) for r in range(grp_count)]
    ).astype(BF16)

    for far, dz, dy in NEAR:
        push(att.at[g], att.at[g], 3 if far == 3 else 5, {"grp": grp_at(dz, dy)})
    big[2].wait()

    def unpack(offsets):
        for dz, dy in offsets:
            home = grp_at(Z - dz, Y - dy)
            both = att[home].astype(F32)
            att_f[home] = both[:heads]
            att_f[grp_at(Z - dz + Z // 2, Y - dy + Y // 2)] = both[heads:]

    closer = [(dz, dy) for far, dz, dy in NEAR if far < 3]
    farthest = [(dz, dy) for far, dz, dy in NEAR if far == 3]
    await_bytes(att, len(closer), recv_sems.at[5])
    unpack([(0, 0)] + closer)
    await_bytes(att, len(farthest), recv_sems.at[3])
    unpack(farthest)
    flat = jnp.concatenate([att_f[:, h, :] for h in range(heads)], axis=1).astype(BF16)
    part = jnp.dot(flat, w[...], preferred_element_type=F32)

    rows = grp_count // 8
    width = part.shape[1] // tp_count
    for p in range(tp_count):
        at = p * width
        tile = jnp.zeros((8, 128), F32)
        for j in range(rows):
            piece = part[8 * j : 8 * j + 8, at // 128 * 128 : at // 128 * 128 + 128]
            shift = (width * j - at) % 128
            if shift:
                piece = pltpu.roll(piece, shift, 1)
            tile = jnp.where(lane // width == j, piece, tile)
        part_out[p] = tile
    part_in[t] = part_out[t]
    for i in tp_order:
        push(part_out.at[tp_peer(i)], part_in.at[t], 4, {"tp": tp_peer(i)})
    await_bytes(q_all, grp_count - 1, send_sems.at[0])
    await_bytes(msg, grp_count - 1, send_sems.at[1])
    await_bytes(stat_out, grp_count - 1, send_sems.at[2])
    await_bytes(att, len(farthest), send_sems.at[3])
    await_bytes(att, len(closer), send_sems.at[5])
    await_bytes(part_out, tp_count - 1, send_sems.at[4])
    await_bytes(part_in, tp_count - 1, recv_sems.at[4])
    tile = tree([part_in[p] for p in range(tp_count)])
    out_ref[...] = jnp.concatenate(
        [tile[:, width * j : width * (j + 1)] for j in range(rows)], axis=0
    ).astype(BF16)


def body(
    queries, new_keys, new_values, key_cache, paged_value_cache, lengths, placement, out_weight
):
    grp_count, tp_count = lax.axis_size("grp"), lax.axis_size("tp")
    slots, _, tokens, head = key_cache.shape
    heads = queries.shape[1]
    requests = lengths.shape[0]
    padded = slots + 16
    return pl.pallas_call(
        functools.partial(kernel, grp_count, tp_count),
        out_shape=pltpu.VMEM((requests, out_weight.shape[1] // tp_count), BF16),
        in_specs=[pl.BlockSpec(memory_space=pltpu.HBM)] * 8,
        out_specs=pl.BlockSpec(memory_space=pltpu.VMEM),
        scratch_shapes=[
            pltpu.VMEM((requests, heads, head), BF16),
            pltpu.VMEM((1, head), BF16),
            pltpu.VMEM((1, head), BF16),
            pltpu.VMEM((slots, tokens, head), BF16),
            pltpu.VMEM((slots, head, tokens), BF16),
            pltpu.VMEM((slots, tokens, head), BF16),
            pltpu.VMEM(out_weight.shape, BF16),
            pltpu.SMEM(lengths.shape, jnp.int32),
            pltpu.SMEM((2, slots), jnp.int32),
            pltpu.VMEM((slots, heads, tokens), F32),
            pltpu.VMEM((requests, heads, head), F32),
            pltpu.VMEM((padded, heads, head), F32),
            pltpu.VMEM((padded, heads, head), F32),
            pltpu.VMEM((requests, heads, head), F32),
            pltpu.VMEM((requests * heads, padded * heads), BF16),
            pltpu.VMEM((requests, 2 * heads, head), BF16),
            pltpu.VMEM((requests, 2 * heads, head), BF16),
            pltpu.VMEM((requests, 1, 128), F32),
            pltpu.VMEM((requests, 1, 128), F32),
            pltpu.VMEM((requests, 2 * heads, head), BF16),
            pltpu.VMEM((requests, heads, head), F32),
            pltpu.VMEM((tp_count, 8, 128), F32),
            pltpu.VMEM((tp_count, 8, 128), F32),
            pltpu.SemaphoreType.DMA((5,)),
            pltpu.SemaphoreType.DMA,
            pltpu.SemaphoreType.DMA,
            pltpu.SemaphoreType.DMA,
            pltpu.SemaphoreType.DMA((6,)),
            pltpu.SemaphoreType.DMA((6,)),
        ],
        compiler_params=pltpu.CompilerParams(
            collective_id=0, has_side_effects=True, vmem_limit_bytes=32 << 20
        ),
    )(
        *(
            pltpu.with_memory_space_constraint(x, pltpu.HBM)
            for x in (
                queries,
                new_keys,
                new_values,
                key_cache.reshape(slots, tokens, head),
                paged_value_cache.reshape(slots, tokens, head),
                lengths,
                placement.T,
                out_weight,
            )
        )
    )


def solution(mesh):
    in_specs = (
        P("grp", "tp", None),
        P("grp", "tp", None),
        P("grp", "tp", None),
        P("grp", "tp", None, None),
        P("grp", "tp", None, None),
        P(),
        P("grp", None),
        P("tp", "grp"),
    )
    out_specs = P(None, ("grp", "tp"))
    return jax.shard_map(body, mesh=mesh, in_specs=in_specs, out_specs=out_specs, check_vma=False)
```
